32 devices in a mesh: ctx: 4 (over y, x), exp: 4 (over z), dp: 2 (over core).
Axes of the slice: x: 2, y: 2, z: 4, core: 2. Of those that a mesh axis runs over, the one named last changes fastest.
Arguments:
- residual: bfloat16 [512, 4096], P('ctx', ('exp', 'dp')), may hold values from -6 to 6
- ssm_values: bfloat16 [512, 4096], P('ctx', ('exp', 'dp')), may hold values from -6 to 6
- ssm_keys: bfloat16 [512, 64], P('ctx'), may hold values from -6 to 6
- ssm_queries: bfloat16 [512, 64], P('ctx'), may hold values from -0.03125 to 0.03125
- log_decay: float32 [512, 64], P('ctx', ('exp', 'dp')), may hold values from -1 to 0, as said below
- expert_ids: int32 [512, 2], P('ctx'), may hold values from 0 to 3, all different within a row; in each aligned block of 128 rows (0 to 127, 128 to 255, ...) at most 80 rows name the same one
- gate_probs: float32 [512, 2], P('ctx'), may hold values from 0.2 to 1
- norm_gain: float32 [4096], P(('exp', 'dp')), may hold values from 0.5 to 1.5
- w_gate: bfloat16 [4, 4096, 8192], P('exp', None, ('ctx', 'dp')), may hold values from -0.09375 to 0.09375
- w_up: bfloat16 [4, 4096, 8192], P('exp', None, ('ctx', 'dp')), may hold values from -0.09375 to 0.09375
- w_down: bfloat16 [4, 4096, 8192], P('exp', None, ('ctx', 'dp')), may hold values from -0.0625 to 0.0625
- out_grad: bfloat16 [512, 4096], P('ctx', ('exp', 'dp')), may hold values from -6 to 6
Outputs:
- grad_residual: bfloat16 [512, 4096], P('ctx', ('exp', 'dp'))
- grad_values: bfloat16 [512, 4096], P('ctx', ('exp', 'dp'))
- grad_keys: float32 [512, 64], P('ctx')
- grad_queries: float32 [512, 64], P('ctx')
- grad_decay: float32 [512, 64], P('ctx', ('exp', 'dp'))
- grad_probs: float32 [512, 2], P('ctx')
- grad_gain: float32 [4096], P(('exp', 'dp'))
- w_gate_grad: bfloat16 [4, 4096, 8192], P('exp', None, ('ctx', 'dp'))
- w_up_grad: bfloat16 [4, 4096, 8192], P('exp', None, ('ctx', 'dp'))
- w_down_grad: bfloat16 [4, 4096, 8192], P('exp', None, ('ctx', 'dp'))
The draws below stay inside these ranges and needn't reach their ends.
Inputs may be any that keep to these rules, and one draw needn't show every extreme that they name: `expert_ids`: each token names two different experts; among the 128 tokens of one index of ctx (aligned blocks) no expert is named more than 80 times, a bound that some block reaches. `log_decay`: negative everywhere.
All inputs are finite; a program needn't handle non-finite values.
Results may differ from the reference program's by a relative error of at most 0.028.
Values may be sent and summed in bfloat16 or wider, within the bound.
A program may use at most 128 MiB of HBM per device.

```python
import math
import jax
import jax.numpy as jnp
import numpy as np
from jax import lax

D = 4096
HEADS = 64
HDIM = 64
STATE = 64
FW = 8192
TOK_DEV = 128
EXPERTS = 4
FW_DEV = 1024
SEQUENCE_LENGTH = 512
CAP = 80
N_CTX = 4


def draw_log_decay(key, part):
    random_subkeys = jax.random.split(key, 7)
    complete_shape = (SEQUENCE_LENGTH, HEADS)
    fast_share = 0.4
    fast_mask = (jax.random.uniform(random_subkeys[0], (1, HEADS)) < fast_share).astype(jnp.float32)
    fast_rate = jnp.exp(jax.random.uniform(random_subkeys[1], (1, HEADS), minval=math.log(1.0 / 50.0), maxval=math.log(1.0 / 30.0)))
    slow_rate = jax.random.uniform(random_subkeys[2], (1, HEADS), minval=0.1, maxval=0.4) * (math.log(10.0) / SEQUENCE_LENGTH)
    baseline_decay_rate = fast_mask * fast_rate + (1.0 - fast_mask) * slow_rate
    blocks = SEQUENCE_LENGTH // TOK_DEV
    block_scale_factor = jnp.exp(jax.random.uniform(random_subkeys[3], (blocks, 1, HEADS), minval=math.log(0.5), maxval=math.log(2.0)))
    block_scale_factor = jnp.broadcast_to(block_scale_factor, (blocks, TOK_DEV, HEADS)).reshape(complete_shape)
    random_noise = jax.random.uniform(random_subkeys[4], complete_shape, minval=0.7, maxval=1.4)
    spike_position = jax.random.randint(random_subkeys[5], (1, 2), 0, SEQUENCE_LENGTH)
    sequence_position = jnp.arange(SEQUENCE_LENGTH, dtype=jnp.int32)[:, None, None]
    spike_selected = jnp.any(sequence_position == spike_position[None], axis=2).astype(jnp.float32)
    spike_log_decay = jnp.log(jax.random.uniform(random_subkeys[6], complete_shape, minval=0.55, maxval=0.8))
    return -baseline_decay_rate * block_scale_factor * random_noise + spike_selected * spike_log_decay


def shard_levels(rng, dims, cuts, smallest, top_value):
    def one(dim, parts):
        steps = jax.random.uniform(jax.random.fold_in(jax.random.fold_in(rng, 6), dim), (parts,), jnp.float32, smallest / len(cuts), top_value / len(cuts))
        return jnp.repeat(jnp.exp(steps), dims[dim] // parts).reshape((-1,) + (1,) * (len(dims) - dim - 1))

    gain = one(*cuts[0])
    for cut in cuts[1:]:
        gain = gain * one(*cut)
    return gain


def assign_block(rng, own, number, rows, count, top, most, slope):
    ranking = jax.random.permutation(rng, count)
    crowded, ordinary = shares(count, rows * top, most, slope, True), shares(count, rows * top, most, slope, False)
    places = jnp.arange(count)

    def named(tallies, rotation):
        used = int((tallies > 0).sum())
        fixed = max(1, used // 4)
        moved = fixed + (places - fixed + rotation * (used - fixed)) % max(1, count - fixed)
        return jnp.zeros((count,), jnp.int32).at[ranking[jnp.where(places < fixed, places, moved)]].set(jnp.asarray(tallies, jnp.int32))

    tallies = jnp.where(number % 4 == 0, named(crowded, number // 4), named(ordinary, number - number // 4 - 1))
    mixed = jax.random.permutation(jax.random.fold_in(own, 3), count)
    giver, sink = mixed[0:count // 2 * 2:2], mixed[1:count // 2 * 2:2]
    room = jnp.minimum(tallies[giver] - 1, most - tallies[sink]) // 2
    room = jnp.where((giver == ranking[0]) | (sink == ranking[0]) | (tallies[sink] == 0), 0, jnp.maximum(room, 0))
    moved = jax.random.randint(jax.random.fold_in(own, 4), (count // 2,), 0, 1 << 20) % (room + 1)
    tallies = tallies.at[giver].add(-moved).at[sink].add(moved)
    items = jnp.searchsorted(jnp.cumsum(tallies), jnp.arange(rows * top), side="right").astype(jnp.int32)
    table = items.reshape(top, rows).T
    table = table[jax.random.permutation(jax.random.fold_in(own, 1), rows)]
    rotation = jax.random.randint(jax.random.fold_in(own, 2), (rows, 1), 0, top)
    return jnp.take_along_axis(table, (jnp.arange(top)[None, :] + rotation) % top, axis=1)


def shares(number_of, total, reach, skew, full):
    loads = [(1 << 20) // math.isqrt(standing ** skew) + 1 for standing in range(1, number_of + 1)]
    largest = reach if full else min(reach, max(-(-total // number_of), total * loads[0] // sum(loads)))
    least = 1 if total - largest >= number_of - 1 else 0
    given, spare = [largest] + [least] * (number_of - 1), total - largest - least * (number_of - 1)
    while spare > 0:
        free = [i for i in range(1, number_of) if given[i] < largest] or [i for i in range(1, number_of) if given[i] < reach]
        whole, remaining = sum([loads[i] for i in free]), spare
        for i in free:
            extra = min(reach - given[i], max(1, remaining * loads[i] // whole), spare)
            given[i] = given[i] + extra
            spare = spare - extra
    return np.array(given)


def normal_values(rng, dims, spread, reach, cuts=(), held_as=jnp.bfloat16):
    values = jax.random.normal(rng, dims, jnp.float32) * spread
    if len(cuts) > 0:
        values = shard_levels(rng, dims, cuts, -0.22, 0.18) * values
    return jnp.clip(values, min=-reach, max=reach).astype(held_as)


def setup_inputs(seed: int = 0) -> dict:
    seeds = jax.random.split(jax.random.key(seed), 13)
    residual = normal_values(seeds[0], (SEQUENCE_LENGTH, D), 1.0, 6.0, ((0, 4), (1, 8)))
    ssm_values = normal_values(seeds[1], (SEQUENCE_LENGTH, D), 1.0, 6.0, ((0, 4), (1, 8)))
    ssm_keys = normal_values(seeds[2], (SEQUENCE_LENGTH, STATE), 1.0, 6.0, ((0, 4),))
    ssm_queries = normal_values(seeds[3], (SEQUENCE_LENGTH, STATE), (STATE * SEQUENCE_LENGTH) ** -0.5, 0.03125, ((0, 4),))
    log_decay = draw_log_decay(jax.random.fold_in(seeds[12], 71), 0)
    expert_ids_keys = jax.random.split(jax.random.fold_in(seeds[5], 1), SEQUENCE_LENGTH // TOK_DEV)
    expert_ids_turns = jax.random.permutation(jax.random.fold_in(seeds[5], 3), SEQUENCE_LENGTH // TOK_DEV)
    expert_ids = jax.vmap(lambda own, number: assign_block(jax.random.fold_in(seeds[5], 2), own, number, TOK_DEV, EXPERTS, 2, CAP, 2))(expert_ids_keys, expert_ids_turns).reshape((SEQUENCE_LENGTH, 2))
    gate_probs = jnp.clip(0.2 + 0.8 * jax.random.uniform(seeds[6], (SEQUENCE_LENGTH, 2), jnp.float32) ** shard_levels(seeds[6], (SEQUENCE_LENGTH, 2), ((0, 4),), -0.2, 0.2), 0.2, 1.0)
    norm_gain = jnp.clip(1.0 + 0.1 * jax.random.normal(seeds[7], (D,), jnp.float32), 0.5, 1.5)
    w_gate = normal_values(seeds[8], (EXPERTS, D, FW), D ** -0.5, 0.09375, ((0, 4), (2, 8)))
    w_up = normal_values(seeds[9], (EXPERTS, D, FW), D ** -0.5, 0.09375, ((0, 4), (2, 8)))
    w_down = normal_values(seeds[10], (EXPERTS, D, FW), FW ** -0.5, 0.0625, ((0, 4), (2, 8)))
    out_grad = normal_values(seeds[11], (SEQUENCE_LENGTH, D), 1.0, 6.0, ((0, 4), (1, 8)))
    return {"residual": residual, "ssm_values": ssm_values, "ssm_keys": ssm_keys, "ssm_queries": ssm_queries, "log_decay": log_decay, "expert_ids": expert_ids, "gate_probs": gate_probs, "norm_gain": norm_gain, "w_gate": w_gate, "w_up": w_up, "w_down": w_down, "out_grad": out_grad}


HIGH = lax.Precision.HIGHEST
EPS = 1e-05

def block_state(values, key_rows, log_decay):
    cumulative = jnp.cumsum(log_decay, axis=0)
    total_log = cumulative[-1]
    tail_decay = jnp.exp(total_log[None, :] - cumulative)
    weighted = tail_decay[:, :, None] * values
    state_local = jnp.einsum('shp,sn->hpn', weighted, key_rows, precision=HIGH)
    return (jnp.exp(total_log), state_local)

def block_output(values, key_rows, queries, log_decay, state_in):
    cumulative = jnp.cumsum(log_decay, axis=0)
    length = values.shape[0]
    row_index = lax.broadcasted_iota(jnp.int32, (length, length), 0)
    col_index = lax.broadcasted_iota(jnp.int32, (length, length), 1)
    causal = (row_index >= col_index)[None]
    cum_heads = cumulative.T
    log_gap = jnp.where(causal, cum_heads[:, :, None] - cum_heads[:, None, :], 0.0)
    decay_mat = jnp.where(causal, jnp.exp(log_gap), 0.0)
    scores = jnp.dot(queries, key_rows.T, precision=HIGH)
    inner_part = jnp.einsum('hts,shp->thp', decay_mat * scores[None], values, precision=HIGH)
    carried = jnp.einsum('tn,hpn->thp', queries, state_in, precision=HIGH)
    return inner_part + jnp.exp(cumulative)[:, :, None] * carried

def silu_parts(gate_act):
    sigmoid_val = jax.nn.sigmoid(gate_act)
    return (gate_act * sigmoid_val, sigmoid_val * (1.0 + gate_act * (1.0 - sigmoid_val)))

def route_slots(token_ids, expert_count):
    owners = token_ids.reshape(-1)
    onehot = (owners[:, None] == jnp.arange(expert_count, dtype=jnp.int32)[None, :]).astype(jnp.int32)
    rank_before = jnp.cumsum(onehot, axis=0) - onehot
    return (owners, lax.optimization_barrier(jnp.sum(rank_before * onehot, axis=1)).astype(jnp.int32))

def seq_output(values, key_rows, queries, log_decay):
    blocks = values.shape[0] // TOK_DEV

    def advance(state_in, pieces):
        block_vals, block_keys, block_queries, block_decay = pieces
        out_rows = block_output(block_vals, block_keys, block_queries, block_decay, state_in)
        decay_total, state_local = block_state(block_vals, block_keys, block_decay)
        return (decay_total[:, None, None] * state_in + state_local, out_rows)
    pieces = (values.reshape(blocks, TOK_DEV, HEADS, HDIM), key_rows.reshape(blocks, TOK_DEV, STATE), queries.reshape(blocks, TOK_DEV, STATE), log_decay.reshape(blocks, TOK_DEV, HEADS))
    start_state = jnp.zeros((HEADS, HDIM, STATE), jnp.float32)
    _, outputs = lax.scan(advance, start_state, pieces)
    return outputs.reshape(-1, HEADS, HDIM)

def grouped_sum(term_of_group, rows, width):
    groups = FW // FW_DEV

    def add_group(running, group):
        start = (group * FW_DEV).astype(jnp.int32)
        term = term_of_group(start)
        rounded = lax.optimization_barrier(term.astype(jnp.bfloat16))
        return (running + rounded.astype(jnp.float32), None)
    start_sum = jnp.zeros((rows, width), jnp.float32)
    total, _ = lax.scan(add_group, start_sum, jnp.arange(groups, dtype=jnp.int32))
    return total

def one_expert(pieces):
    got_rows, got_cot, gate_w, up_w, down_w = pieces
    rows = got_rows.shape[0]
    act_gate = jnp.dot(got_rows, gate_w, preferred_element_type=jnp.float32)
    act_up = jnp.dot(got_rows, up_w, preferred_element_type=jnp.float32)
    swish_val, swish_slope = silu_parts(act_gate)
    hidden_act = (swish_val * act_up).astype(jnp.bfloat16)

    def out_term(start):
        part_act = lax.dynamic_slice_in_dim(hidden_act, start, FW_DEV, 1)
        weight = lax.dynamic_slice_in_dim(down_w, start, FW_DEV, 1)
        return jnp.dot(part_act, weight.T, preferred_element_type=jnp.float32)
    expert_out = grouped_sum(out_term, rows, D).astype(jnp.bfloat16)
    grad_act = jnp.dot(got_cot, down_w, preferred_element_type=jnp.float32)
    grad_gate = (grad_act * act_up * swish_slope).astype(jnp.bfloat16)
    grad_up = (grad_act * swish_val).astype(jnp.bfloat16)

    def back_term(start):
        part_gate = lax.dynamic_slice_in_dim(grad_gate, start, FW_DEV, 1)
        part_up = lax.dynamic_slice_in_dim(grad_up, start, FW_DEV, 1)
        weight_gate = lax.dynamic_slice_in_dim(gate_w, start, FW_DEV, 1)
        weight_up = lax.dynamic_slice_in_dim(up_w, start, FW_DEV, 1)
        return jnp.dot(part_gate, weight_gate.T, preferred_element_type=jnp.float32) + jnp.dot(part_up, weight_up.T, preferred_element_type=jnp.float32)
    pair_back = grouped_sum(back_term, rows, D).astype(jnp.bfloat16)
    gate_grad = jnp.dot(got_rows.T, grad_gate, preferred_element_type=jnp.float32).astype(jnp.bfloat16)
    up_grad = jnp.dot(got_rows.T, grad_up, preferred_element_type=jnp.float32).astype(jnp.bfloat16)
    down_grad = jnp.dot(got_cot.T, hidden_act, preferred_element_type=jnp.float32).astype(jnp.bfloat16)
    return (expert_out, pair_back, gate_grad, up_grad, down_grad)

def reference(residual, ssm_values, ssm_keys, ssm_queries, log_decay, expert_ids, gate_probs, norm_gain, w_gate, w_up, w_down, out_grad):
    seq_values = ssm_values.astype(jnp.float32).reshape(SEQUENCE_LENGTH, HEADS, HDIM)
    seq_keys = ssm_keys.astype(jnp.float32)
    seq_queries = ssm_queries.astype(jnp.float32)
    mixer_out = seq_output(seq_values, seq_keys, seq_queries, log_decay)
    hidden = (residual.astype(jnp.float32) + mixer_out.reshape(SEQUENCE_LENGTH, D)).astype(jnp.bfloat16)
    hidden_f = hidden.astype(jnp.float32)
    inv_rms = lax.rsqrt(lax.optimization_barrier(jnp.mean(hidden_f * hidden_f, axis=1, keepdims=True)) + EPS)
    normed = (hidden_f * inv_rms * norm_gain).astype(jnp.bfloat16)
    block_ids = expert_ids.reshape(N_CTX, TOK_DEV, 2)
    owners, slot_index = jax.vmap(lambda ids_block: route_slots(ids_block, EXPERTS))(block_ids)
    ctx_number = lax.broadcasted_iota(jnp.int32, owners.shape, 0)
    flat_row = ctx_number * CAP + slot_index
    pair_rows = jnp.repeat(normed.reshape(N_CTX, TOK_DEV, D), 2, axis=1)
    dout_rows = jnp.repeat(out_grad.reshape(N_CTX, TOK_DEV, D), 2, axis=1)
    pair_prob = gate_probs.reshape(N_CTX, 2 * TOK_DEV)
    pair_cot = (pair_prob[..., None] * dout_rows.astype(jnp.float32)).astype(jnp.bfloat16)
    empty = jnp.zeros((EXPERTS, N_CTX * CAP, D), jnp.bfloat16)
    rows_buffer = empty.at[owners, flat_row].set(pair_rows)
    cot_buffer = empty.at[owners, flat_row].set(pair_cot)
    out_buffer, back_buffer, w_gate_grad, w_up_grad, w_down_grad = lax.map(one_expert, (rows_buffer, cot_buffer, w_gate, w_up, w_down))
    out_pairs = out_buffer[owners, flat_row]
    grad_probs = lax.optimization_barrier(jnp.sum(out_pairs.astype(jnp.float32) * dout_rows.astype(jnp.float32), axis=2)).reshape(SEQUENCE_LENGTH, 2)
    back_pairs = back_buffer[owners, flat_row].astype(jnp.float32)
    grad_normed = back_pairs.reshape(N_CTX, TOK_DEV, 2, D).sum(axis=2).reshape(SEQUENCE_LENGTH, D)
    scaled = grad_normed * norm_gain
    projection = lax.optimization_barrier(jnp.mean(hidden_f * scaled, axis=1, keepdims=True))
    grad_hidden = out_grad.astype(jnp.float32) + inv_rms * scaled - hidden_f * inv_rms ** 3 * projection
    grad_gain = lax.optimization_barrier(jnp.sum(grad_normed * hidden_f * inv_rms, axis=0))
    grad_residual = grad_hidden.astype(jnp.bfloat16)
    _, pull_back = jax.vjp(seq_output, seq_values, seq_keys, seq_queries, log_decay)
    values_grad, grad_keys, grad_queries, grad_decay = pull_back(grad_hidden.reshape(SEQUENCE_LENGTH, HEADS, HDIM))
    grad_values = values_grad.reshape(SEQUENCE_LENGTH, D).astype(jnp.bfloat16)
    return (grad_residual, grad_values, grad_keys, grad_queries, grad_decay, grad_probs, grad_gain, w_gate_grad, w_up_grad, w_down_grad)
```

```python
import jax
import jax.numpy as jnp
from jax import lax
from jax.sharding import PartitionSpec as P

HIGH = lax.Precision.HIGHEST
EPS = 1e-05


def entering(x, axis, join, neutral):
    place = lax.axis_index(axis)
    gathered = jax.tree.map(
        lambda a, kind: lax.all_gather(a.astype(kind), axis), x, (jnp.bfloat16, jnp.bfloat16)
    )
    state = jax.tree.map(lambda a, e: jnp.zeros_like(a) + jnp.asarray(e, a.dtype), x, neutral)

    def entering_one(step, state):
        return join(
            state,
            jax.tree.map(
                lambda a, own: lax.dynamic_index_in_dim(a, step, 0, False).astype(own.dtype),
                gathered,
                x,
            ),
        )

    return lax.fori_loop(0, place, entering_one, state)


def carried_in(x, axis, join, neutral):
    count = lax.axis_size(axis)
    place = lax.axis_index(axis)
    ahead = count - 1 - place
    gathered = jax.tree.map(
        lambda a, kind: lax.all_gather(a.astype(kind), axis),
        x,
        jax.tree.map(lambda a: jnp.bfloat16 if a.dtype == jnp.float32 else a.dtype, x),
    )
    state = jax.tree.map(lambda a, e: jnp.zeros_like(a) + jnp.asarray(e, a.dtype), x, neutral)

    def carried_one(step, state):
        source = count - 1 - step
        return join(
            state,
            jax.tree.map(
                lambda a, own: lax.dynamic_index_in_dim(a, source, 0, False).astype(own.dtype),
                gathered,
                x,
            ),
        )

    return lax.fori_loop(0, ahead, carried_one, state)


def running_sum(x):
    length = x.shape[0]
    row_index = lax.broadcasted_iota(jnp.int32, (length, length), 0)
    col_index = lax.broadcasted_iota(jnp.int32, (length, length), 1)
    lower = (row_index >= col_index).astype(jnp.float32)
    return jnp.dot(lower, x, precision=HIGH)


def block_state(values, key_rows, log_decay):
    cumulative = running_sum(log_decay)
    total_log = cumulative[-1]
    tail_decay = jnp.exp(total_log[None, :] - cumulative)
    weighted = tail_decay[:, :, None] * values
    state_local = jnp.einsum("shp,sn->hpn", weighted, key_rows, precision=HIGH)
    return (jnp.exp(total_log), state_local)


def block_output(values, key_rows, queries, log_decay, state_in):
    cumulative = running_sum(log_decay)
    length = values.shape[0]
    row_index = lax.broadcasted_iota(jnp.int32, (length, length), 0)
    col_index = lax.broadcasted_iota(jnp.int32, (length, length), 1)
    causal = (row_index >= col_index)[None]
    cum_heads = cumulative.T
    log_gap = jnp.where(causal, cum_heads[:, :, None] - cum_heads[:, None, :], 0.0)
    decay_mat = jnp.where(causal, jnp.exp(log_gap), 0.0)
    scores = jnp.dot(queries, key_rows.T, precision=HIGH)
    inner_part = jnp.einsum("hts,shp->thp", decay_mat * scores[None], values, precision=HIGH)
    carried = jnp.einsum("tn,hpn->thp", queries, state_in, precision=HIGH)
    return inner_part + jnp.exp(cumulative)[:, :, None] * carried


def silu_parts(gate_act):
    sigmoid_val = jax.nn.sigmoid(gate_act)
    return (gate_act * sigmoid_val, sigmoid_val * (1.0 + gate_act * (1.0 - sigmoid_val)))


def route_slots(token_ids, expert_count):
    owners = token_ids.reshape(-1)
    onehot = (owners[:, None] == jnp.arange(expert_count, dtype=jnp.int32)[None, :]).astype(
        jnp.int32
    )
    rank_before = running_sum(onehot.astype(jnp.float32)).astype(jnp.int32) - onehot
    return (owners, jnp.sum(rank_before * onehot, axis=1))


def combine_states(earlier_part, later_part):
    return (
        earlier_part[0] * later_part[0],
        later_part[0][:, None, None] * earlier_part[1] + later_part[1],
    )


def arrange_rows(gathered, ctx_count, dp_count):
    capacity = gathered.shape[1]
    exp_count = gathered.shape[2]
    feat = gathered.shape[3]
    shaped = gathered.reshape(ctx_count, dp_count, capacity, exp_count, feat)
    return shaped.transpose(0, 2, 3, 1, 4).reshape(
        ctx_count * capacity, exp_count * dp_count * feat
    )


def arrange_sums(full_term, ctx_count, dp_count, exp_count, capacity):
    feat = full_term.shape[1] // (exp_count * dp_count)
    shaped = full_term.reshape(ctx_count, capacity, exp_count, dp_count, feat)
    return shaped.transpose(0, 3, 1, 2, 4).reshape(
        ctx_count * dp_count * capacity, exp_count * feat
    )


def per_device(
    residual,
    ssm_values,
    ssm_keys,
    ssm_queries,
    log_decay,
    expert_ids,
    gate_probs,
    norm_gain,
    w_gate,
    w_up,
    w_down,
    out_grad,
):
    tokens = residual.shape[0]
    feat = residual.shape[1]
    heads_here = log_decay.shape[1]
    head_size = feat // heads_here
    model_width = w_gate.shape[1]
    ctx_count = lax.axis_size("ctx")
    exp_count = lax.axis_size("exp")
    dp_count = lax.axis_size("dp")
    expert_count = w_gate.shape[0] * exp_count
    capacity = 5 * tokens // (2 * expert_count)
    block_vals = ssm_values.astype(jnp.float32).reshape(tokens, heads_here, head_size)
    block_keys = ssm_keys.astype(jnp.float32)
    block_queries = ssm_queries.astype(jnp.float32)
    (decay_total, state_local), state_pull = jax.vjp(block_state, block_vals, block_keys, log_decay)
    neutral = (jnp.ones_like(decay_total), jnp.zeros_like(state_local))
    state_in = entering((decay_total, state_local), "ctx", combine_states, neutral)[1]
    mixer_out, output_pull = jax.vjp(
        block_output, block_vals, block_keys, block_queries, log_decay, state_in
    )
    hidden = (residual.astype(jnp.float32) + mixer_out.reshape(tokens, feat)).astype(jnp.bfloat16)
    hidden_f = hidden.astype(jnp.float32)
    square_sum = lax.psum(jnp.sum(hidden_f * hidden_f, axis=1), ("exp", "dp"))
    inv_rms = lax.rsqrt(square_sum / model_width + EPS)[:, None]
    normed = (hidden_f * inv_rms * norm_gain[None, :]).astype(jnp.bfloat16)
    owners, slot_index = route_slots(expert_ids, expert_count)
    pair_rows = jnp.repeat(normed, 2, axis=0)
    dout_rows = jnp.repeat(out_grad, 2, axis=0)
    pair_prob = gate_probs.reshape(-1)
    pair_cot = (pair_prob[:, None] * dout_rows.astype(jnp.float32)).astype(jnp.bfloat16)
    empty = jnp.zeros((expert_count, capacity, feat), jnp.bfloat16)
    send_rows = empty.at[owners, slot_index].set(pair_rows).reshape(expert_count, capacity, 1, feat)
    got_rows = lax.all_to_all(send_rows, "exp", split_axis=0, concat_axis=2, tiled=True)
    all_rows = lax.all_gather(got_rows, ("ctx", "dp"), axis=0, tiled=True)
    rows_flat = arrange_rows(all_rows, ctx_count, dp_count)
    act_gate = jnp.dot(rows_flat, w_gate[0], preferred_element_type=jnp.float32)
    act_up = jnp.dot(rows_flat, w_up[0], preferred_element_type=jnp.float32)
    swish_val, swish_slope = silu_parts(act_gate)
    hidden_act = (swish_val * act_up).astype(jnp.bfloat16)
    full_out = lax.dot_general(
        hidden_act, w_down[0], (((1,), (1,)), ((), ())), preferred_element_type=jnp.float32
    )
    out_total = lax.psum_scatter(
        arrange_sums(full_out, ctx_count, dp_count, exp_count, capacity).astype(jnp.bfloat16),
        ("ctx", "dp"),
        scatter_dimension=0,
        tiled=True,
    )
    expert_out = out_total.reshape(1, capacity, exp_count, feat)
    back_out = lax.all_to_all(expert_out, "exp", split_axis=2, concat_axis=0, tiled=True).reshape(
        expert_count, capacity, feat
    )
    out_pairs = back_out[owners, slot_index]
    probs_part = jnp.einsum(
        "kd,kd->k", out_pairs, dout_rows, preferred_element_type=jnp.float32
    ).reshape(tokens, 2)
    grad_probs = lax.psum(probs_part, ("exp", "dp"))
    send_cot = empty.at[owners, slot_index].set(pair_cot).reshape(expert_count, capacity, 1, feat)
    got_cot = lax.all_to_all(send_cot, "exp", split_axis=0, concat_axis=2, tiled=True)
    all_cot = lax.all_gather(got_cot, ("ctx", "dp"), axis=0, tiled=True)
    cot_flat = arrange_rows(all_cot, ctx_count, dp_count)
    grad_act = jnp.dot(cot_flat, w_down[0], preferred_element_type=jnp.float32)
    grad_gate = (grad_act * act_up * swish_slope).astype(jnp.bfloat16)
    grad_up = (grad_act * swish_val).astype(jnp.bfloat16)
    full_back = lax.dot_general(
        grad_gate, w_gate[0], (((1,), (1,)), ((), ())), preferred_element_type=jnp.float32
    ) + lax.dot_general(
        grad_up, w_up[0], (((1,), (1,)), ((), ())), preferred_element_type=jnp.float32
    )
    back_total = lax.psum_scatter(
        arrange_sums(full_back, ctx_count, dp_count, exp_count, capacity).astype(jnp.bfloat16),
        ("ctx", "dp"),
        scatter_dimension=0,
        tiled=True,
    )
    pair_back = back_total.reshape(1, capacity, exp_count, feat)
    back_in = lax.all_to_all(pair_back, "exp", split_axis=2, concat_axis=0, tiled=True).reshape(
        expert_count, capacity, feat
    )
    grad_normed = (
        back_in[owners, slot_index].astype(jnp.float32).reshape(tokens, 2, feat).sum(axis=1)
    )
    w_gate_grad = jnp.dot(rows_flat.T, grad_gate, preferred_element_type=jnp.float32).astype(
        jnp.bfloat16
    )[None]
    w_up_grad = jnp.dot(rows_flat.T, grad_up, preferred_element_type=jnp.float32).astype(
        jnp.bfloat16
    )[None]
    w_down_grad = jnp.dot(cot_flat.T, hidden_act, preferred_element_type=jnp.float32).astype(
        jnp.bfloat16
    )[None]
    scaled = grad_normed * norm_gain[None, :]
    inner_sum = lax.psum(jnp.sum(hidden_f * scaled, axis=1), ("exp", "dp"))
    projection = (inner_sum / model_width)[:, None]
    grad_hidden = (
        out_grad.astype(jnp.float32) + inv_rms * scaled - hidden_f * inv_rms**3 * projection
    )
    gain_part = jnp.sum(grad_normed * hidden_f * inv_rms, axis=0)
    grad_gain = lax.psum(gain_part, "ctx")
    grad_mixer = grad_hidden.reshape(tokens, heads_here, head_size)
    vals_first, keys_first, queries_part, decay_first, carry_cot = output_pull(grad_mixer)
    grad_state = carried_in((decay_total, carry_cot), "ctx", combine_states, neutral)[1]
    grad_total = jnp.sum(grad_state * state_in, axis=(1, 2))
    vals_second, keys_second, decay_second = state_pull((grad_total, grad_state))
    grad_keys, grad_queries = (
        lax.psum((keys_first + keys_second).astype(jnp.bfloat16), ("exp", "dp")).astype(
            jnp.float32
        ),
        lax.psum(queries_part.astype(jnp.bfloat16), ("exp", "dp")).astype(jnp.float32),
    )
    grad_residual = grad_hidden.astype(jnp.bfloat16)
    grad_values = (vals_first + vals_second).reshape(tokens, feat).astype(jnp.bfloat16)
    grad_decay = decay_first + decay_second
    return (
        grad_residual,
        grad_values,
        grad_keys,
        grad_queries,
        grad_decay,
        grad_probs,
        grad_gain,
        w_gate_grad,
        w_up_grad,
        w_down_grad,
    )


def solution(mesh):
    return jax.shard_map(
        per_device,
        mesh=mesh,
        in_specs=(
            P("ctx", ("exp", "dp")),
            P("ctx", ("exp", "dp")),
            P("ctx", None),
            P("ctx", None),
            P("ctx", ("exp", "dp")),
            P("ctx", None),
            P("ctx", None),
            P(("exp", "dp")),
            P("exp", None, ("ctx", "dp")),
            P("exp", None, ("ctx", "dp")),
            P("exp", None, ("ctx", "dp")),
            P("ctx", ("exp", "dp")),
        ),
        out_specs=(
            P("ctx", ("exp", "dp")),
            P("ctx", ("exp", "dp")),
            P("ctx", None),
            P("ctx", None),
            P("ctx", ("exp", "dp")),
            P("ctx", None),
            P(("exp", "dp")),
            P("exp", None, ("ctx", "dp")),
            P("exp", None, ("ctx", "dp")),
            P("exp", None, ("ctx", "dp")),
        ),
        check_vma=False,
    )
```

```python
import jax
import jax.numpy as jnp
from jax import lax
from jax.sharding import PartitionSpec as P

HIGH = lax.Precision.HIGHEST
EPS = 1e-05


def pass_along(gathered, decays, forward):
    count = lax.axis_size("ctx")
    place = lax.axis_index("ctx")
    state = jnp.zeros(gathered.shape[1:], jnp.float32)
    for step in range(count - 1):
        source = step if forward else count - 1 - step
        joined = decays[source][:, None, None] * state + gathered[source].astype(jnp.float32)
        state = jnp.where(source < place if forward else source > place, joined, state)
    return state


def two_parts(x):
    high = lax.reduce_precision(x, 8, 7)
    return (high.astype(jnp.bfloat16), (x - high).astype(jnp.bfloat16))


def sum_over(x, axes):
    return jnp.sum(lax.all_gather(x, axes).astype(jnp.float32), axis=0)


def running_sum(x):
    length = x.shape[0]
    row_index = lax.broadcasted_iota(jnp.int32, (length, length), 0)
    col_index = lax.broadcasted_iota(jnp.int32, (length, length), 1)
    lower = (row_index >= col_index).astype(jnp.float32)
    return jnp.dot(lower, x, precision=HIGH)


def block_state(values, key_rows, log_decay):
    cumulative = running_sum(log_decay)
    total_log = cumulative[-1]
    tail_decay = jnp.exp(total_log[None, :] - cumulative)
    weighted = tail_decay[:, :, None] * values
    state_local = jnp.einsum("shp,sn->hpn", weighted, key_rows, precision=HIGH)
    return (jnp.exp(total_log), state_local)


def block_output(values, key_rows, queries, log_decay, state_in):
    cumulative = running_sum(log_decay)
    length = values.shape[0]
    row_index = lax.broadcasted_iota(jnp.int32, (length, length), 0)
    col_index = lax.broadcasted_iota(jnp.int32, (length, length), 1)
    causal = (row_index >= col_index)[None]
    cum_heads = cumulative.T
    log_gap = jnp.where(causal, cum_heads[:, :, None] - cum_heads[:, None, :], 0.0)
    decay_mat = jnp.where(causal, jnp.exp(log_gap), 0.0)
    scores = jnp.dot(queries, key_rows.T, precision=HIGH)
    inner_part = jnp.einsum("hts,shp->thp", decay_mat * scores[None], values, precision=HIGH)
    carried = jnp.einsum("tn,hpn->thp", queries, state_in, precision=HIGH)
    return inner_part + jnp.exp(cumulative)[:, :, None] * carried


def silu_parts(gate_act):
    sigmoid_val = jax.nn.sigmoid(gate_act)
    return (gate_act * sigmoid_val, sigmoid_val * (1.0 + gate_act * (1.0 - sigmoid_val)))


def route_slots(token_ids, expert_count):
    owners = token_ids.reshape(-1)
    onehot = (owners[:, None] == jnp.arange(expert_count, dtype=jnp.int32)[None, :]).astype(
        jnp.int32
    )
    rank_before = running_sum(onehot.astype(jnp.float32)).astype(jnp.int32) - onehot
    return (owners, jnp.sum(rank_before * onehot, axis=1))


def arrange_rows(gathered, ctx_count, dp_count):
    exp_count, capacity, feat = gathered.shape[1:]
    shaped = gathered.reshape(ctx_count, dp_count, exp_count, capacity, feat)
    return shaped.transpose(0, 3, 2, 1, 4).reshape(
        ctx_count * capacity, exp_count * dp_count * feat
    )


def arrange_sums(full_term, ctx_count, dp_count, exp_count, capacity):
    feat = full_term.shape[1] // (exp_count * dp_count)
    shaped = full_term.reshape(ctx_count, capacity, exp_count, dp_count, feat)
    return shaped.transpose(0, 3, 2, 1, 4).reshape(-1, feat)


def expert_rows(rows, expert_count, ctx_count, dp_count):
    send = rows.reshape(expert_count, -1, rows.shape[1])
    got = lax.all_to_all(send, "exp", split_axis=0, concat_axis=0, tiled=True)
    return arrange_rows(lax.all_gather(got, ("ctx", "dp")), ctx_count, dp_count)


def token_rows(full_term, ctx_count, dp_count, exp_count, capacity):
    total = lax.psum_scatter(
        arrange_sums(full_term, ctx_count, dp_count, exp_count, capacity),
        ("ctx", "dp"),
        scatter_dimension=0,
        tiled=True,
    )
    feat = total.shape[1]
    back = lax.all_to_all(
        total.reshape(exp_count, capacity, feat), "exp", split_axis=0, concat_axis=0, tiled=True
    )
    return back.reshape(-1, feat)


def rows_back(select, rows):
    return lax.dot_general(
        select, rows, (((0,), (0,)), ((), ())), preferred_element_type=jnp.float32
    )


def per_device(
    residual,
    ssm_values,
    ssm_keys,
    ssm_queries,
    log_decay,
    expert_ids,
    gate_probs,
    norm_gain,
    w_gate,
    w_up,
    w_down,
    out_grad,
):
    tokens = residual.shape[0]
    feat = residual.shape[1]
    heads_here = log_decay.shape[1]
    head_size = feat // heads_here
    model_width = w_gate.shape[1]
    ctx_count = lax.axis_size("ctx")
    exp_count = lax.axis_size("exp")
    dp_count = lax.axis_size("dp")
    expert_count = w_gate.shape[0] * exp_count
    capacity = 5 * tokens // (2 * expert_count)
    block_vals = ssm_values.astype(jnp.float32).reshape(tokens, heads_here, head_size)
    block_keys = ssm_keys.astype(jnp.float32)
    block_queries = ssm_queries.astype(jnp.float32)
    (decay_total, state_local), state_pull = jax.vjp(block_state, block_vals, block_keys, log_decay)
    decay_row = jnp.broadcast_to(decay_total[:, None, None], state_local[:, :1].shape)
    spans = lax.all_gather(
        jnp.concatenate([state_local, decay_row], axis=1).astype(jnp.bfloat16), "ctx"
    )
    decays = spans[:, :, -1, 0].astype(jnp.float32)
    state_in = pass_along(spans[:, :, :-1], decays, True)
    mixer_out, output_pull = jax.vjp(
        block_output, block_vals, block_keys, block_queries, log_decay, state_in
    )
    hidden = (residual.astype(jnp.float32) + mixer_out.reshape(tokens, feat)).astype(jnp.bfloat16)
    hidden_f = hidden.astype(jnp.float32)
    square_sum = sum_over(jnp.sum(hidden_f * hidden_f, axis=1), ("exp", "dp"))
    inv_rms = lax.rsqrt(square_sum / model_width + EPS)[:, None]
    normed = (hidden_f * inv_rms * norm_gain[None, :]).astype(jnp.bfloat16)
    owners, slot_index = route_slots(expert_ids, expert_count)
    row_of = (owners * capacity + slot_index).reshape(tokens, 2)
    row_number = lax.broadcasted_iota(jnp.int32, (expert_count * capacity, tokens), 0)
    first = row_number == row_of[:, 0][None, :]
    second = row_number == row_of[:, 1][None, :]
    select = (first | second).astype(jnp.bfloat16)
    row_prob = jnp.sum(
        jnp.where(first, gate_probs[:, 0][None, :], 0.0)
        + jnp.where(second, gate_probs[:, 1][None, :], 0.0),
        axis=1,
    )
    cot_rows = jnp.dot(select, out_grad, preferred_element_type=jnp.float32)
    cot_rows = (row_prob[:, None] * cot_rows).astype(jnp.bfloat16)
    cot_flat = expert_rows(cot_rows, expert_count, ctx_count, dp_count)
    send_rows = jnp.dot(select, normed, preferred_element_type=jnp.float32).astype(jnp.bfloat16)
    rows_flat = expert_rows(send_rows, expert_count, ctx_count, dp_count)
    act_gate = jnp.dot(rows_flat, w_gate[0], preferred_element_type=jnp.float32)
    act_up = jnp.dot(rows_flat, w_up[0], preferred_element_type=jnp.float32)
    swish_val, swish_slope = silu_parts(act_gate)
    hidden_act = (swish_val * act_up).astype(jnp.bfloat16)
    grad_act = jnp.dot(cot_flat, w_down[0], preferred_element_type=jnp.float32)
    grad_gate = (grad_act * act_up * swish_slope).astype(jnp.bfloat16)
    grad_up = (grad_act * swish_val).astype(jnp.bfloat16)
    full_back = lax.dot_general(
        grad_gate, w_gate[0], (((1,), (1,)), ((), ())), preferred_element_type=jnp.float32
    ) + lax.dot_general(
        grad_up, w_up[0], (((1,), (1,)), ((), ())), preferred_element_type=jnp.float32
    )
    full_back, later_act = lax.optimization_barrier((full_back.astype(jnp.bfloat16), hidden_act))
    back_in = token_rows(full_back, ctx_count, dp_count, exp_count, capacity)
    full_out = lax.dot_general(
        later_act, w_down[0], (((1,), (1,)), ((), ())), preferred_element_type=jnp.float32
    )
    back_out = token_rows(full_out.astype(jnp.bfloat16), ctx_count, dp_count, exp_count, capacity)
    grad_normed = rows_back(select, back_in)
    out_f = out_grad.astype(jnp.float32)
    probs_part = jnp.stack(
        [
            jnp.sum(rows_back(first.astype(jnp.bfloat16), back_out) * out_f, axis=1),
            jnp.sum(rows_back(second.astype(jnp.bfloat16), back_out) * out_f, axis=1),
        ]
    )
    w_gate_grad = jnp.dot(rows_flat.T, grad_gate, preferred_element_type=jnp.float32).astype(
        jnp.bfloat16
    )[None]
    w_up_grad = jnp.dot(rows_flat.T, grad_up, preferred_element_type=jnp.float32).astype(
        jnp.bfloat16
    )[None]
    w_down_grad = jnp.dot(cot_flat.T, hidden_act, preferred_element_type=jnp.float32).astype(
        jnp.bfloat16
    )[None]
    scaled = grad_normed * norm_gain[None, :]
    inner_sum = sum_over(jnp.sum(hidden_f * scaled, axis=1), ("exp", "dp"))
    projection = (inner_sum / model_width)[:, None]
    grad_hidden = (
        out_grad.astype(jnp.float32) + inv_rms * scaled - hidden_f * inv_rms**3 * projection
    )
    gain_part = jnp.sum(grad_normed * hidden_f * inv_rms, axis=0)
    grad_mixer = grad_hidden.reshape(tokens, heads_here, head_size)
    vals_first, keys_first, queries_part, decay_first, carry_cot = output_pull(grad_mixer)
    width = state_local.shape[2]
    gain_rows = [p.reshape(heads_here, -1, width) for p in two_parts(gain_part)]
    carries = lax.all_gather(
        jnp.concatenate([carry_cot.astype(jnp.bfloat16)] + gain_rows, axis=1), "ctx"
    )
    grad_state = pass_along(carries[:, :, :head_size], decays, False)
    gain_high, gain_low = jnp.split(
        jnp.sum(carries[:, :, head_size:].astype(jnp.float32), axis=0), 2, axis=1
    )
    grad_gain = (gain_high + gain_low).reshape(feat)
    grad_total = jnp.sum(grad_state * state_in, axis=(1, 2))
    vals_second, keys_second, decay_second = state_pull((grad_total, grad_state))
    both = jnp.concatenate([keys_first + keys_second, queries_part], axis=1).astype(jnp.bfloat16)
    probs_rows = jnp.concatenate(two_parts(probs_part)).reshape(-1, both.shape[1])
    summed = sum_over(jnp.concatenate([both, probs_rows]), ("exp", "dp"))
    grad_keys, grad_queries = summed[:tokens, :width], summed[:tokens, width:]
    probs_high, probs_low = jnp.split(summed[tokens:].reshape(4, tokens), 2)
    grad_probs = (probs_high + probs_low).T
    grad_residual = grad_hidden.astype(jnp.bfloat16)
    grad_values = (vals_first + vals_second).reshape(tokens, feat).astype(jnp.bfloat16)
    grad_decay = decay_first + decay_second
    return (
        grad_residual,
        grad_values,
        grad_keys,
        grad_queries,
        grad_decay,
        grad_probs,
        grad_gain,
        w_gate_grad,
        w_up_grad,
        w_down_grad,
    )


def solution(mesh):
    return jax.shard_map(
        per_device,
        mesh=mesh,
        in_specs=(
            P("ctx", ("exp", "dp")),
            P("ctx", ("exp", "dp")),
            P("ctx", None),
            P("ctx", None),
            P("ctx", ("exp", "dp")),
            P("ctx", None),
            P("ctx", None),
            P(("exp", "dp")),
            P("exp", None, ("ctx", "dp")),
            P("exp", None, ("ctx", "dp")),
            P("exp", None, ("ctx", "dp")),
            P("ctx", ("exp", "dp")),
        ),
        out_specs=(
            P("ctx", ("exp", "dp")),
            P("ctx", ("exp", "dp")),
            P("ctx", None),
            P("ctx", None),
            P("ctx", ("exp", "dp")),
            P("ctx", None),
            P(("exp", "dp")),
            P("exp", None, ("ctx", "dp")),
            P("exp", None, ("ctx", "dp")),
            P("exp", None, ("ctx", "dp")),
        ),
        check_vma=False,
    )
```

```python
import jax
import jax.numpy as jnp
from jax import lax
from jax.sharding import PartitionSpec as P

HIGH = lax.Precision.HIGHEST
EPS = 1e-05


def pass_along(gathered, decays, forward):
    count = lax.axis_size("ctx")
    place = lax.axis_index("ctx")
    state = jnp.zeros(gathered.shape[1:], jnp.float32)
    for step in range(count - 1):
        source = step if forward else count - 1 - step
        joined = decays[source][:, None, None] * state + gathered[source].astype(jnp.float32)
        state = jnp.where(source < place if forward else source > place, joined, state)
    return state


def two_parts(x):
    high = lax.reduce_precision(x, 8, 7)
    return (high.astype(jnp.bfloat16), (x - high).astype(jnp.bfloat16))


def sum_over(x, axes):
    return jnp.sum(lax.all_gather(x, axes).astype(jnp.float32), axis=0)


def running_sum(x):
    length = x.shape[0]
    row_index = lax.broadcasted_iota(jnp.int32, (length, length), 0)
    col_index = lax.broadcasted_iota(jnp.int32, (length, length), 1)
    lower = (row_index >= col_index).astype(jnp.float32)
    return jnp.dot(lower, x, precision=HIGH)


def block_state(values, key_rows, log_decay):
    cumulative = running_sum(log_decay)
    total_log = cumulative[-1]
    tail_decay = jnp.exp(total_log[None, :] - cumulative)
    weighted = tail_decay[:, :, None] * values
    state_local = jnp.einsum("shp,sn->hpn", weighted, key_rows, precision=HIGH)
    return (jnp.exp(total_log), state_local)


def block_output(values, key_rows, queries, log_decay, state_in):
    cumulative = running_sum(log_decay)
    length = values.shape[0]
    row_index = lax.broadcasted_iota(jnp.int32, (length, length), 0)
    col_index = lax.broadcasted_iota(jnp.int32, (length, length), 1)
    causal = (row_index >= col_index)[None]
    cum_heads = cumulative.T
    log_gap = jnp.where(causal, cum_heads[:, :, None] - cum_heads[:, None, :], 0.0)
    decay_mat = jnp.where(causal, jnp.exp(log_gap), 0.0)
    scores = jnp.dot(queries, key_rows.T, precision=HIGH)
    inner_part = jnp.einsum("hts,shp->thp", decay_mat * scores[None], values, precision=HIGH)
    carried = jnp.einsum("tn,hpn->thp", queries, state_in, precision=HIGH)
    return inner_part + jnp.exp(cumulative)[:, :, None] * carried


def silu_parts(gate_act):
    sigmoid_val = jax.nn.sigmoid(gate_act)
    return (gate_act * sigmoid_val, sigmoid_val * (1.0 + gate_act * (1.0 - sigmoid_val)))


def route_slots(token_ids, expert_count):
    owners = token_ids.reshape(-1)
    onehot = (owners[:, None] == jnp.arange(expert_count, dtype=jnp.int32)[None, :]).astype(
        jnp.int32
    )
    rank_before = running_sum(onehot.astype(jnp.float32)).astype(jnp.int32) - onehot
    return (owners, jnp.sum(rank_before * onehot, axis=1))


def arrange_rows(gathered, ctx_count, dp_count):
    exp_count, capacity, feat = gathered.shape[1:]
    shaped = gathered.reshape(ctx_count, dp_count, exp_count, capacity, feat)
    blocks = [
        shaped[:, d, e].reshape(ctx_count * capacity, feat)
        for e in range(exp_count)
        for d in range(dp_count)
    ]
    return jnp.concatenate(blocks, axis=1)


def arrange_sums(full_term, ctx_count, dp_count, exp_count, capacity):
    feat = full_term.shape[1] // (exp_count * dp_count)
    shaped = full_term.reshape(ctx_count, capacity, -1)
    starts = [(e * dp_count + d) * feat for d in range(dp_count) for e in range(exp_count)]
    blocks = [shaped[:, None, :, start : start + feat] for start in starts]
    return jnp.concatenate(blocks, axis=1).reshape(-1, feat)


def expert_rows(rows, expert_count, ctx_count, dp_count):
    send = rows.reshape(expert_count, -1, rows.shape[1])
    got = lax.all_to_all(send, "exp", split_axis=0, concat_axis=0, tiled=True)
    return arrange_rows(lax.all_gather(got, ("ctx", "dp")), ctx_count, dp_count)


def summed_rows(full_term, ctx_count, dp_count, exp_count, capacity):
    return lax.psum_scatter(
        arrange_sums(full_term, ctx_count, dp_count, exp_count, capacity),
        ("ctx", "dp"),
        scatter_dimension=0,
        tiled=True,
    )


def token_rows(total, exp_count):
    feat = total.shape[1]
    back = lax.all_to_all(
        total.reshape(exp_count, -1, feat), "exp", split_axis=0, concat_axis=0, tiled=True
    )
    return back.reshape(-1, feat)


def rows_back(select, rows):
    return lax.dot_general(
        select, rows, (((0,), (0,)), ((), ())), preferred_element_type=jnp.float32
    )


def per_device(
    residual,
    ssm_values,
    ssm_keys,
    ssm_queries,
    log_decay,
    expert_ids,
    gate_probs,
    norm_gain,
    w_gate,
    w_up,
    w_down,
    out_grad,
):
    tokens = residual.shape[0]
    feat = residual.shape[1]
    heads_here = log_decay.shape[1]
    head_size = feat // heads_here
    model_width = w_gate.shape[1]
    ctx_count = lax.axis_size("ctx")
    exp_count = lax.axis_size("exp")
    dp_count = lax.axis_size("dp")
    expert_count = w_gate.shape[0] * exp_count
    capacity = 5 * tokens // (2 * expert_count)
    block_vals = ssm_values.astype(jnp.float32).reshape(tokens, heads_here, head_size)
    block_keys = ssm_keys.astype(jnp.float32)
    block_queries = ssm_queries.astype(jnp.float32)
    (decay_total, state_local), state_pull = jax.vjp(block_state, block_vals, block_keys, log_decay)
    decay_row = jnp.broadcast_to(decay_total[:, None, None], state_local[:, :1].shape)
    spans = lax.all_gather(
        jnp.concatenate([state_local, decay_row], axis=1).astype(jnp.bfloat16), "ctx"
    )
    decays = spans[:, :, -1, 0].astype(jnp.float32)
    state_in = pass_along(spans[:, :, :-1], decays, True)
    mixer_out, output_pull = jax.vjp(
        block_output, block_vals, block_keys, block_queries, log_decay, state_in
    )
    hidden = (residual.astype(jnp.float32) + mixer_out.reshape(tokens, feat)).astype(jnp.bfloat16)
    hidden_f = hidden.astype(jnp.float32)
    square_sum = sum_over(jnp.sum(hidden_f * hidden_f, axis=1), ("exp", "dp"))
    inv_rms = lax.rsqrt(square_sum / model_width + EPS)[:, None]
    normed = (hidden_f * inv_rms * norm_gain[None, :]).astype(jnp.bfloat16)
    owners, slot_index = route_slots(expert_ids, expert_count)
    row_of = (owners * capacity + slot_index).reshape(tokens, 2)
    row_number = lax.broadcasted_iota(jnp.int32, (expert_count * capacity, tokens), 0)
    first = row_number == row_of[:, 0][None, :]
    second = row_number == row_of[:, 1][None, :]
    select = (first | second).astype(jnp.bfloat16)
    row_prob = jnp.sum(
        jnp.where(first, gate_probs[:, 0][None, :], 0.0)
        + jnp.where(second, gate_probs[:, 1][None, :], 0.0),
        axis=1,
    )
    cot_rows = jnp.dot(select, out_grad, preferred_element_type=jnp.float32)
    cot_rows = (row_prob[:, None] * cot_rows).astype(jnp.bfloat16)
    cot_flat = expert_rows(cot_rows, expert_count, ctx_count, dp_count)
    send_rows = jnp.dot(select, normed, preferred_element_type=jnp.float32).astype(jnp.bfloat16)
    rows_flat = expert_rows(send_rows, expert_count, ctx_count, dp_count)
    act_gate = jnp.dot(rows_flat, w_gate[0], preferred_element_type=jnp.float32)
    act_up = jnp.dot(rows_flat, w_up[0], preferred_element_type=jnp.float32)
    swish_val, swish_slope = silu_parts(act_gate)
    hidden_act = (swish_val * act_up).astype(jnp.bfloat16)
    grad_act = jnp.dot(cot_flat, w_down[0], preferred_element_type=jnp.float32)
    grad_gate = (grad_act * act_up * swish_slope).astype(jnp.bfloat16)
    grad_up = (grad_act * swish_val).astype(jnp.bfloat16)
    full_back = lax.dot_general(
        grad_gate, w_gate[0], (((1,), (1,)), ((), ())), preferred_element_type=jnp.float32
    ) + lax.dot_general(
        grad_up, w_up[0], (((1,), (1,)), ((), ())), preferred_element_type=jnp.float32
    )
    full_back, later_act = lax.optimization_barrier((full_back.astype(jnp.bfloat16), hidden_act))
    back_total = summed_rows(full_back, ctx_count, dp_count, exp_count, capacity)
    back_in = token_rows(back_total, exp_count)
    full_out = lax.dot_general(
        later_act, w_down[0], (((1,), (1,)), ((), ())), preferred_element_type=jnp.float32
    )
    out_total = summed_rows(
        full_out.astype(jnp.bfloat16), ctx_count, dp_count, exp_count, capacity
    )
    grad_normed = rows_back(select, back_in)
    out_f = out_grad.astype(jnp.float32)
    w_gate_grad = jnp.dot(rows_flat.T, grad_gate, preferred_element_type=jnp.float32).astype(
        jnp.bfloat16
    )[None]
    w_up_grad = jnp.dot(rows_flat.T, grad_up, preferred_element_type=jnp.float32).astype(
        jnp.bfloat16
    )[None]
    w_down_grad = jnp.dot(cot_flat.T, hidden_act, preferred_element_type=jnp.float32).astype(
        jnp.bfloat16
    )[None]
    scaled = grad_normed * norm_gain[None, :]
    inner_sum = sum_over(jnp.sum(hidden_f * scaled, axis=1), ("exp", "dp"))
    projection = (inner_sum / model_width)[:, None]
    grad_hidden = (
        out_grad.astype(jnp.float32) + inv_rms * scaled - hidden_f * inv_rms**3 * projection
    )
    gain_part = jnp.sum(grad_normed * hidden_f * inv_rms, axis=0)
    grad_mixer = grad_hidden.reshape(tokens, heads_here, head_size)
    vals_first, keys_first, queries_part, decay_first, carry_cot = output_pull(grad_mixer)
    width = state_local.shape[2]
    gain_rows = [p.reshape(heads_here, -1, width) for p in two_parts(gain_part)]
    carries = lax.all_gather(
        jnp.concatenate([carry_cot.astype(jnp.bfloat16)] + gain_rows, axis=1), "ctx"
    )
    grad_state = pass_along(carries[:, :, :head_size], decays, False)
    gain_high, gain_low = jnp.split(
        jnp.sum(carries[:, :, head_size:].astype(jnp.float32), axis=0), 2, axis=1
    )
    grad_gain = (gain_high + gain_low).reshape(feat)
    grad_state, out_total = lax.optimization_barrier((grad_state, out_total))
    back_out = token_rows(out_total, exp_count)
    probs_part = jnp.stack(
        [
            jnp.sum(rows_back(first.astype(jnp.bfloat16), back_out) * out_f, axis=1),
            jnp.sum(rows_back(second.astype(jnp.bfloat16), back_out) * out_f, axis=1),
        ]
    )
    grad_total = jnp.sum(grad_state * state_in, axis=(1, 2))
    vals_second, keys_second, decay_second = state_pull((grad_total, grad_state))
    both = jnp.concatenate([keys_first + keys_second, queries_part], axis=1).astype(jnp.bfloat16)
    probs_rows = jnp.concatenate(two_parts(probs_part)).reshape(-1, both.shape[1])
    summed = sum_over(jnp.concatenate([both, probs_rows]), ("exp", "dp"))
    grad_keys, grad_queries = summed[:tokens, :width], summed[:tokens, width:]
    probs_high, probs_low = jnp.split(summed[tokens:].reshape(4, tokens), 2)
    grad_probs = (probs_high + probs_low).T
    grad_residual = grad_hidden.astype(jnp.bfloat16)
    grad_values = (vals_first + vals_second).reshape(tokens, feat).astype(jnp.bfloat16)
    grad_decay = decay_first + decay_second
    return (
        grad_residual,
        grad_values,
        grad_keys,
        grad_queries,
        grad_decay,
        grad_probs,
        grad_gain,
        w_gate_grad,
        w_up_grad,
        w_down_grad,
    )


def solution(mesh):
    return jax.shard_map(
        per_device,
        mesh=mesh,
        in_specs=(
            P("ctx", ("exp", "dp")),
            P("ctx", ("exp", "dp")),
            P("ctx", None),
            P("ctx", None),
            P("ctx", ("exp", "dp")),
            P("ctx", None),
            P("ctx", None),
            P(("exp", "dp")),
            P("exp", None, ("ctx", "dp")),
            P("exp", None, ("ctx", "dp")),
            P("exp", None, ("ctx", "dp")),
            P("ctx", ("exp", "dp")),
        ),
        out_specs=(
            P("ctx", ("exp", "dp")),
            P("ctx", ("exp", "dp")),
            P("ctx", None),
            P("ctx", None),
            P("ctx", ("exp", "dp")),
            P("ctx", None),
            P(("exp", "dp")),
            P("exp", None, ("ctx", "dp")),
            P("exp", None, ("ctx", "dp")),
            P("exp", None, ("ctx", "dp")),
        ),
        check_vma=False,
    )
```

```python
import jax
import jax.numpy as jnp
from jax import lax
from jax.sharding import PartitionSpec as P

HIGH = lax.Precision.HIGHEST
EPS = 1e-05


def pass_along(gathered, decays, forward):
    count = lax.axis_size("ctx")
    place = lax.axis_index("ctx")
    state = jnp.zeros(gathered.shape[1:], jnp.float32)
    for step in range(count - 1):
        source = step if forward else count - 1 - step
        joined = decays[source][:, None, None] * state + gathered[source].astype(jnp.float32)
        state = jnp.where(source < place if forward else source > place, joined, state)
    return state


def two_parts(x):
    high = lax.reduce_precision(x, 8, 7)
    return (high.astype(jnp.bfloat16), (x - high).astype(jnp.bfloat16))


def sum_over(x, axes):
    return jnp.sum(lax.all_gather(x, axes).astype(jnp.float32), axis=0)


def running_sum(x):
    length = x.shape[0]
    row_index = lax.broadcasted_iota(jnp.int32, (length, length), 0)
    col_index = lax.broadcasted_iota(jnp.int32, (length, length), 1)
    lower = (row_index >= col_index).astype(jnp.float32)
    return jnp.dot(lower, x, precision=HIGH)


def block_state(values, key_rows, log_decay):
    cumulative = running_sum(log_decay)
    total_log = cumulative[-1]
    tail_decay = jnp.exp(total_log[None, :] - cumulative)
    weighted = tail_decay[:, :, None] * values
    state_local = jnp.einsum("shp,sn->hpn", weighted, key_rows, precision=HIGH)
    return (jnp.exp(total_log), state_local)


def block_output(values, key_rows, queries, log_decay, state_in):
    cumulative = running_sum(log_decay)
    length = values.shape[0]
    row_index = lax.broadcasted_iota(jnp.int32, (length, length), 0)
    col_index = lax.broadcasted_iota(jnp.int32, (length, length), 1)
    causal = (row_index >= col_index)[None]
    cum_heads = cumulative.T
    log_gap = jnp.where(causal, cum_heads[:, :, None] - cum_heads[:, None, :], 0.0)
    decay_mat = jnp.where(causal, jnp.exp(log_gap), 0.0)
    scores = jnp.dot(queries, key_rows.T, precision=HIGH)
    inner_part = jnp.einsum("hts,shp->thp", decay_mat * scores[None], values, precision=HIGH)
    carried = jnp.einsum("tn,hpn->thp", queries, state_in, precision=HIGH)
    return inner_part + jnp.exp(cumulative)[:, :, None] * carried


def silu_parts(gate_act):
    sigmoid_val = jax.nn.sigmoid(gate_act)
    return (gate_act * sigmoid_val, sigmoid_val * (1.0 + gate_act * (1.0 - sigmoid_val)))


def route_slots(token_ids, expert_count):
    owners = token_ids.reshape(-1)
    onehot = (owners[:, None] == jnp.arange(expert_count, dtype=jnp.int32)[None, :]).astype(
        jnp.int32
    )
    rank_before = running_sum(onehot.astype(jnp.float32)).astype(jnp.int32) - onehot
    return (owners, jnp.sum(rank_before * onehot, axis=1))


def arrange_rows(gathered, ctx_count, dp_count):
    exp_count, capacity, feat = gathered.shape[1:]
    shaped = gathered.reshape(ctx_count, dp_count, exp_count, capacity, feat)
    blocks = [
        shaped[:, d, e].reshape(ctx_count * capacity, feat)
        for e in range(exp_count)
        for d in range(dp_count)
    ]
    return jnp.concatenate(blocks, axis=1)


def arrange_sums(full_term, ctx_count, dp_count, exp_count, capacity):
    feat = full_term.shape[1] // (exp_count * dp_count)
    shaped = full_term.reshape(ctx_count, capacity, -1)
    starts = [(e * dp_count + d) * feat for d in range(dp_count) for e in range(exp_count)]
    blocks = [shaped[:, None, :, start : start + feat] for start in starts]
    return jnp.concatenate(blocks, axis=1).reshape(-1, feat)


def expert_rows(rows, expert_count, ctx_count, dp_count):
    send = rows.reshape(expert_count, -1, rows.shape[1])
    got = lax.all_to_all(send, "exp", split_axis=0, concat_axis=0, tiled=True)
    return (got, arrange_rows(lax.all_gather(got, ("ctx", "dp")), ctx_count, dp_count))


def summed_rows(full_term, ctx_count, dp_count, exp_count, capacity):
    return lax.psum_scatter(
        arrange_sums(full_term, ctx_count, dp_count, exp_count, capacity),
        ("ctx", "dp"),
        scatter_dimension=0,
        tiled=True,
    )


def token_rows(total, exp_count):
    feat = total.shape[1]
    back = lax.all_to_all(
        total.reshape(exp_count, -1, feat), "exp", split_axis=0, concat_axis=0, tiled=True
    )
    return back.reshape(-1, feat)


def rows_back(select, rows):
    return lax.dot_general(
        select, rows, (((0,), (0,)), ((), ())), preferred_element_type=jnp.float32
    )


def per_device(
    residual,
    ssm_values,
    ssm_keys,
    ssm_queries,
    log_decay,
    expert_ids,
    gate_probs,
    norm_gain,
    w_gate,
    w_up,
    w_down,
    out_grad,
):
    tokens = residual.shape[0]
    feat = residual.shape[1]
    heads_here = log_decay.shape[1]
    head_size = feat // heads_here
    model_width = w_gate.shape[1]
    ctx_count = lax.axis_size("ctx")
    exp_count = lax.axis_size("exp")
    dp_count = lax.axis_size("dp")
    expert_count = w_gate.shape[0] * exp_count
    capacity = 5 * tokens // (2 * expert_count)
    block_vals = ssm_values.astype(jnp.float32).reshape(tokens, heads_here, head_size)
    block_keys = ssm_keys.astype(jnp.float32)
    block_queries = ssm_queries.astype(jnp.float32)
    (decay_total, state_local), state_pull = jax.vjp(block_state, block_vals, block_keys, log_decay)
    decay_row = jnp.broadcast_to(decay_total[:, None, None], state_local[:, :1].shape)
    spans = lax.all_gather(
        jnp.concatenate([state_local, decay_row], axis=1).astype(jnp.bfloat16), "ctx"
    )
    decays = spans[:, :, -1, 0].astype(jnp.float32)
    state_in = pass_along(spans[:, :, :-1], decays, True)
    mixer_out, output_pull = jax.vjp(
        block_output, block_vals, block_keys, block_queries, log_decay, state_in
    )
    hidden = (residual.astype(jnp.float32) + mixer_out.reshape(tokens, feat)).astype(jnp.bfloat16)
    hidden_f = hidden.astype(jnp.float32)
    square_sum = sum_over(jnp.sum(hidden_f * hidden_f, axis=1), ("exp", "dp"))
    inv_rms = lax.rsqrt(square_sum / model_width + EPS)[:, None]
    normed = (hidden_f * inv_rms * norm_gain[None, :]).astype(jnp.bfloat16)
    owners, slot_index = route_slots(expert_ids, expert_count)
    row_of = (owners * capacity + slot_index).reshape(tokens, 2)
    row_number = lax.broadcasted_iota(jnp.int32, (expert_count * capacity, tokens), 0)
    first = row_number == row_of[:, 0][None, :]
    second = row_number == row_of[:, 1][None, :]
    select = (first | second).astype(jnp.bfloat16)
    row_prob = jnp.sum(
        jnp.where(first, gate_probs[:, 0][None, :], 0.0)
        + jnp.where(second, gate_probs[:, 1][None, :], 0.0),
        axis=1,
    )
    cot_rows = jnp.dot(select, out_grad, preferred_element_type=jnp.float32)
    cot_rows = (row_prob[:, None] * cot_rows).astype(jnp.bfloat16)
    got_cot, cot_flat = expert_rows(cot_rows, expert_count, ctx_count, dp_count)
    send_rows = jnp.dot(select, normed, preferred_element_type=jnp.float32).astype(jnp.bfloat16)
    _, rows_flat = expert_rows(send_rows, expert_count, ctx_count, dp_count)
    act_gate = jnp.dot(rows_flat, w_gate[0], preferred_element_type=jnp.float32)
    act_up = jnp.dot(rows_flat, w_up[0], preferred_element_type=jnp.float32)
    swish_val, swish_slope = silu_parts(act_gate)
    hidden_act = (swish_val * act_up).astype(jnp.bfloat16)
    grad_act = jnp.dot(cot_flat, w_down[0], preferred_element_type=jnp.float32)
    grad_gate = (grad_act * act_up * swish_slope).astype(jnp.bfloat16)
    grad_up = (grad_act * swish_val).astype(jnp.bfloat16)
    full_back = lax.dot_general(
        grad_gate, w_gate[0], (((1,), (1,)), ((), ())), preferred_element_type=jnp.float32
    ) + lax.dot_general(
        grad_up, w_up[0], (((1,), (1,)), ((), ())), preferred_element_type=jnp.float32
    )
    full_back, later_act = lax.optimization_barrier((full_back.astype(jnp.bfloat16), hidden_act))
    back_total = summed_rows(full_back, ctx_count, dp_count, exp_count, capacity)
    back_in = token_rows(back_total, exp_count)
    full_out = lax.dot_general(
        later_act, w_down[0], (((1,), (1,)), ((), ())), preferred_element_type=jnp.float32
    )
    out_total = summed_rows(
        full_out.astype(jnp.bfloat16), ctx_count, dp_count, exp_count, capacity
    )
    grad_normed = rows_back(select, back_in)
    w_gate_grad = jnp.dot(rows_flat.T, grad_gate, preferred_element_type=jnp.float32).astype(
        jnp.bfloat16
    )[None]
    w_up_grad = jnp.dot(rows_flat.T, grad_up, preferred_element_type=jnp.float32).astype(
        jnp.bfloat16
    )[None]
    w_down_grad = jnp.dot(cot_flat.T, hidden_act, preferred_element_type=jnp.float32).astype(
        jnp.bfloat16
    )[None]
    scaled = grad_normed * norm_gain[None, :]
    inner_sum = sum_over(jnp.sum(hidden_f * scaled, axis=1), ("exp", "dp"))
    projection = (inner_sum / model_width)[:, None]
    grad_hidden = (
        out_grad.astype(jnp.float32) + inv_rms * scaled - hidden_f * inv_rms**3 * projection
    )
    gain_part = jnp.sum(grad_normed * hidden_f * inv_rms, axis=0)
    grad_mixer = grad_hidden.reshape(tokens, heads_here, head_size)
    vals_first, keys_first, queries_part, decay_first, carry_cot = output_pull(grad_mixer)
    width = state_local.shape[2]
    gain_rows = [p.reshape(heads_here, -1, width) for p in two_parts(gain_part)]
    carries = lax.all_gather(
        jnp.concatenate([carry_cot.astype(jnp.bfloat16)] + gain_rows, axis=1), "ctx"
    )
    grad_state = pass_along(carries[:, :, :head_size], decays, False)
    gain_high, gain_low = jnp.split(
        jnp.sum(carries[:, :, head_size:].astype(jnp.float32), axis=0), 2, axis=1
    )
    grad_gain = (gain_high + gain_low).reshape(feat)
    grad_state, out_total = lax.optimization_barrier((grad_state, out_total))
    probs_part = jnp.sum(
        out_total.reshape(got_cot.shape).astype(jnp.float32) * got_cot.astype(jnp.float32),
        axis=(0, 2),
    )
    grad_total = jnp.sum(grad_state * state_in, axis=(1, 2))
    vals_second, keys_second, decay_second = state_pull((grad_total, grad_state))
    both = jnp.concatenate([keys_first + keys_second, queries_part], axis=1).astype(jnp.bfloat16)
    probs_flat = jnp.concatenate(two_parts(probs_part))
    probs_flat = jnp.pad(probs_flat, (0, -probs_flat.shape[0] % both.shape[1]))
    ends = lax.all_gather(
        jnp.concatenate([both, probs_flat.reshape(-1, both.shape[1])]), ("exp", "dp")
    ).astype(jnp.float32)
    summed = jnp.sum(ends[:, :tokens], axis=0)
    grad_keys, grad_queries = summed[:, :width], summed[:, width:]
    parts = ends[:, tokens:].reshape(exp_count, dp_count, -1)[:, :, : 2 * capacity]
    parts = parts.reshape(exp_count, dp_count, 2, capacity).sum(axis=(1, 2)).reshape(-1, 1)
    pair_sums = [jnp.sum(jnp.where(m, parts, 0.0), axis=0) for m in (first, second)]
    grad_probs = jnp.stack(pair_sums, axis=1) / gate_probs
    grad_residual = grad_hidden.astype(jnp.bfloat16)
    grad_values = (vals_first + vals_second).reshape(tokens, feat).astype(jnp.bfloat16)
    grad_decay = decay_first + decay_second
    return (
        grad_residual,
        grad_values,
        grad_keys,
        grad_queries,
        grad_decay,
        grad_probs,
        grad_gain,
        w_gate_grad,
        w_up_grad,
        w_down_grad,
    )


def solution(mesh):
    return jax.shard_map(
        per_device,
        mesh=mesh,
        in_specs=(
            P("ctx", ("exp", "dp")),
            P("ctx", ("exp", "dp")),
            P("ctx", None),
            P("ctx", None),
            P("ctx", ("exp", "dp")),
            P("ctx", None),
            P("ctx", None),
            P(("exp", "dp")),
            P("exp", None, ("ctx", "dp")),
            P("exp", None, ("ctx", "dp")),
            P("exp", None, ("ctx", "dp")),
            P("ctx", ("exp", "dp")),
        ),
        out_specs=(
            P("ctx", ("exp", "dp")),
            P("ctx", ("exp", "dp")),
            P("ctx", None),
            P("ctx", None),
            P("ctx", ("exp", "dp")),
            P("ctx", None),
            P(("exp", "dp")),
            P("exp", None, ("ctx", "dp")),
            P("exp", None, ("ctx", "dp")),
            P("exp", None, ("ctx", "dp")),
        ),
        check_vma=False,
    )
```
